512 devices in a mesh: tm: 8 (over x, y_lo), space: 64 (over z, y_hi, core).
Axes of the slice: x: 4, y: 8 (y_hi: 4, y_lo: 2; y = y_hi * 2 + y_lo), z: 8, core: 2. Of those that a mesh axis runs over, the one named last changes fastest.
Arguments:
- lam: float32 [8, 72, 512, 256], P('tm', None, 'space'), may hold values from -6 to 6
- obs_mult: float32 [8, 16384], P('tm', 'space'), may hold values from -6 to 6
- dx: float32 [8, 72, 512, 256], P('tm', None, 'space'), may hold values from -6 to 6
- fresh_state: float32 [2, 72, 512, 256], P(None, None, 'space'), may hold values from -6 to 6
- fresh_obs: float32 [16384], P('space'), may hold values from -6 to 6
- sigma: float32 [8, 72], P('tm'), may hold values from 0.3 to 3
- obs_var: float32 [16384], P('space'), may hold values from 0.5 to 2
- obs_idx: int32 [16384], P('space'), may hold values from 0 to 147455
- stencil_coef: float32 [3, 512, 256], P(None, 'space'), may hold values from 0.05 to 0.25
- vert_cov: float32 [72, 72], replicated, may hold values from -0.75 to 0.75
- block_pattern: int32 [9, 9], replicated, may hold values 0 or 1
Outputs:
- out_lam: float32 [8, 72, 512, 256], P('tm', None, 'space')
- out_obs: float32 [8, 16384], P('tm', 'space')
- out_dx: float32 [8, 72, 512, 256], P('tm', None, 'space')
The draws below stay inside these ranges and needn't reach their ends.
Inputs may be any that keep to these rules, and one draw needn't show every extreme that they name: `obs_idx`: a row-major index (level, row, column) into the observation's tile of 72 x 8 x 256 cells.
All inputs are finite; a program needn't handle non-finite values.
Results may differ from the reference program's by a relative error of at most 0.00007.
Values sent between devices are 32-bit elements; how exact they have to be, the bound alone decides.
A program may use at most 64 MiB of HBM per device.

```python
import math
import jax
import jax.numpy as jnp
from jax import lax

LEV = 72
LB = 8
STEPS = 2
HY = 8
HX = 256
NOBS_DEV = 256
NB = 9
SUBW = 8
NY = 512
NOBS = 16384


def touch_ends(array, own_key, least, top_value):
    dims = array.shape
    index_at = [jax.random.randint(jax.random.fold_in(own_key, axis), (), 0, dims[axis]) for axis in range(len(dims))]
    array = array.at[tuple(index_at)].set(least)
    longest = dims.index(max(dims))
    index_at[longest] = (index_at[longest] + 1) % dims[longest]
    return array.at[tuple(index_at)].set(top_value)


def shard_levels(rng, dims, pieces, low, high):
    def one(position, shards_of):
        heights = jax.random.uniform(jax.random.fold_in(jax.random.fold_in(rng, 6), position), (shards_of,), jnp.float32, low / len(pieces), high / len(pieces))
        return jnp.repeat(jnp.exp(heights), dims[position] // shards_of).reshape((-1,) + (1,) * (len(dims) - position - 1))

    gain = one(*pieces[0])
    for cut in pieces[1:]:
        gain = gain * one(*cut)
    return gain


def normal_values(own_key, extent, scale, reach, cuts=(), held_as=jnp.bfloat16):
    factor_of = shard_levels(own_key, extent, cuts, -0.22, 0.18) if cuts else 1.0
    array = jax.random.normal(own_key, extent, jnp.float32) * scale * factor_of
    return jnp.minimum(jnp.maximum(array, -reach), reach).astype(held_as)


def setup_inputs(seed: int = 0) -> dict:
    seeds = jax.random.split(jax.random.key(seed), 12)
    return {
        "lam": normal_values(seeds[0], (SUBW, LEV, NY, HX), 1.0, 6.0, ((0, 8), (2, 64)), jnp.float32),
        "obs_mult": normal_values(seeds[1], (SUBW, NOBS), 1.0, 6.0, ((0, 8), (1, 64)), jnp.float32),
        "dx": normal_values(seeds[2], (SUBW, LEV, NY, HX), 1.0, 6.0, ((0, 8), (2, 64)), jnp.float32),
        "fresh_state": normal_values(seeds[3], (2, LEV, NY, HX), 1.0, 6.0, ((2, 64),), jnp.float32),
        "fresh_obs": normal_values(seeds[4], (NOBS,), 1.0, 6.0, ((0, 64),), jnp.float32),
        "sigma": jnp.clip(jnp.exp(math.log(3.0) - 2.3025851 * jax.random.uniform(seeds[5], (SUBW, LEV), jnp.float32) ** shard_levels(seeds[5], (SUBW, LEV), ((0, 8),), -0.2, 0.2)), 0.3, 3.0),
        "obs_var": jnp.clip(jnp.exp(math.log(2.0) - 1.3862944 * jax.random.uniform(seeds[6], (NOBS,), jnp.float32) ** shard_levels(seeds[6], (NOBS,), ((0, 64),), -0.2, 0.2)), 0.5, 2.0),
        "obs_idx": touch_ends(jax.random.randint(seeds[7], (NOBS,), 0, LEV * HY * HX), jax.random.fold_in(seeds[7], 1), 0, (LEV * HY * HX) - 1).astype(jnp.int32),
        "stencil_coef": jnp.clip(0.05 + 0.2 * jax.random.uniform(seeds[8], (3, NY, HX), jnp.float32) ** shard_levels(seeds[8], (3, NY, HX), ((1, 64),), -0.2, 0.2), 0.05, 0.25),
        "vert_cov": normal_values(seeds[9], (LEV, LEV), LEV ** -0.5, 0.75, (), jnp.float32),
        "block_pattern": touch_ends((jax.random.randint(seeds[10], (NB, NB), 0, 2) < 1).astype(jnp.int32), jax.random.fold_in(seeds[10], 1), 0, 1),
    }


def pad_rows(v, width):
    return jnp.pad(v, ((0, 0), (0, 0), (width, width), (0, 0)))


def tl_step(v, coef):
    ext = pad_rows(v, 2)
    return v + coef[0] * (ext[:, :, 3:-1] + ext[:, :, 1:-3] - 2.0 * v) + coef[1] * (ext[:, :, 4:] + ext[:, :, :-4] - 2.0 * v) + coef[2] * (jnp.roll(v, 1, axis=3) - v)


def adj_step(u, coef):
    near = pad_rows(coef[0] * u, 2)
    far_rows = pad_rows(coef[1] * u, 2)
    cols = coef[2] * u
    return u + (near[:, :, 3:-1] + near[:, :, 1:-3] - 2.0 * near[:, :, 2:-2]) + (far_rows[:, :, 4:] + far_rows[:, :, :-4] - 2.0 * far_rows[:, :, 2:-2]) + (jnp.roll(cols, -1, axis=3) - cols)


def forward_model(v, coef):
    for step in range(STEPS):
        v = tl_step(v, coef)
    return v


def adjoint_model(u, coef):
    for step in range(STEPS):
        u = adj_step(u, coef)
    return u


def covariance(lam, sigma, vert_cov, block_pattern):
    scale = sigma[:, :, None, None]
    scaled = scale * lam
    ext = pad_rows(scaled, 1)
    smooth = scaled + 0.1 * ((ext[:, :, 2:] + ext[:, :, :-2] - 2.0 * scaled) + (jnp.roll(scaled, 1, axis=3) + jnp.roll(scaled, -1, axis=3) - 2.0 * scaled))
    blocks = jnp.maximum(block_pattern, jnp.eye(NB, dtype=jnp.int32))
    keep = jnp.repeat(jnp.repeat(blocks, LB, axis=0), LB, axis=1).astype(jnp.float32)
    vertical = 2.0 * jnp.eye(LEV, dtype=jnp.float32) + keep * vert_cov
    return scale * jnp.einsum("lm,smyx->slyx", vertical, smooth, precision=lax.Precision.HIGHEST)


def locate(obs_idx):
    tile = jnp.arange(NOBS, dtype=jnp.int32) // NOBS_DEV
    level = obs_idx // (HY * HX)
    rest = obs_idx % (HY * HX)
    return level, tile * HY + rest // HX, rest % HX


def saddle(lam, mult, dx, sigma, obs_var, where, coef, vert_cov, block_pattern):
    level, row, column = where
    moved = forward_model(dx, coef)
    tl_term = jnp.concatenate([jnp.zeros_like(moved[:1]), moved[:-1]], axis=0)
    back = adjoint_model(lam, coef)
    ad_term = jnp.concatenate([back[1:], jnp.zeros_like(back[:1])], axis=0)
    p_lam = covariance(lam, sigma, vert_cov, block_pattern) + (dx - tl_term)
    p_mu = obs_var[None, :] * mult + dx[:, level, row, column]
    spread = jnp.zeros_like(dx).at[:, level, row, column].add(mult)
    p_dx = (lam - ad_term) + spread
    return p_lam, p_mu, p_dx


def reference(lam, obs_mult, dx, fresh_state, fresh_obs, sigma, obs_var, obs_idx, stencil_coef, vert_cov, block_pattern):
    where = locate(obs_idx)
    p_lam, p_mu, p_dx = saddle(lam, obs_mult, dx, sigma, obs_var, where, stencil_coef, vert_cov, block_pattern)
    lam_two = jnp.concatenate([p_lam[1:], fresh_state[0][None]], axis=0)
    dx_two = jnp.concatenate([p_dx[1:], fresh_state[1][None]], axis=0)
    mu_two = jnp.concatenate([p_mu[1:], fresh_obs[None]], axis=0)
    out_lam, out_obs, out_dx = saddle(lam_two, mu_two, dx_two, sigma, obs_var, where, stencil_coef, vert_cov, block_pattern)
    return out_lam, out_obs, out_dx
```

```python
import jax
import jax.numpy as jnp
from jax import lax
from jax.experimental import pallas as pl
from jax.experimental.pallas import tpu as pltpu
from jax.sharding import PartitionSpec as P

MESH = pl.DeviceIdType.MESH
F32 = jnp.float32
BF16 = jnp.bfloat16
LB = 8
NC = 3
GROUP = 4
CHUNKED = ("LC", "LT", "LB", "XC", "XT", "XB", "A", "E", "P", "B", "PT", "PB", "QT", "QB", "OL", "OX")
SINGLE = ("CC", "CT", "CB", "AUX", "F0", "F1", "MU", "OO")
SLOT = {name: i * NC for i, name in enumerate(CHUNKED)}
SLOT.update({name: len(CHUNKED) * NC + i for i, name in enumerate(SINGLE)})
NSEM = len(CHUNKED) * NC + len(SINGLE)


def halves(v):
    high = v.astype(BF16)
    return high, (v - high.astype(F32)).astype(BF16)


def kernel(
    lam, mult, dx, fresh, fobs, sigma, ovar, oidx, coef, vert, pattern,
    out_lam, out_obs, out_dx,
    ring_l, ring_x, ring_p, ring_q, ring_c, cen,
    a_buf, a_in, e_buf, e_in, m_buf, n_buf, b_buf, b_in, d2_in, dl, ht, ol_buf, ox_buf,
    aux, aux_in, mu_buf, mu_in, oo_buf, v3, onehot, ssem, rsem,
):
    levels, rows, cols = a_buf.shape
    nobs = oo_buf.shape[1]
    tms, sps = lax.axis_size("tm"), lax.axis_size("space")
    tm, sp = lax.axis_index("tm"), lax.axis_index("space")
    yl, c = lax.rem(tm, 2), lax.rem(sp, 2)
    rk, rt = tm - yl + c, sp - c + yl
    swapped = yl != c

    def at_role(k, t):
        kb, tb = lax.rem(k + 2, 2), lax.rem(t + 2, 2)
        return (k - kb + tb, t - tb + kb)

    partner = at_role(tm, sp)
    not_first_t, not_last_t = rt > 0, rt < sps - 1
    not_first_k, not_last_k = rk > 0, rk < tms - 1
    fresh_out = jnp.logical_and(tm == tms - 2, c == 0)
    fresh_far = jnp.logical_and(tm == tms - 2, c == 1)
    fresh_own = jnp.logical_and(tm == tms - 1, c == 1)
    links = {
        "swap": (partner, swapped, partner, swapped),
        "araw_top": (at_role(tm, sp - 1), sp > 0, (rk, rt + 1), not_last_t),
        "araw_bot": (at_role(tm, sp + 1), sp < sps - 1, (rk, rt - 1), not_first_t),
        "top": (at_role(rk, rt - 1), not_first_t, at_role(rk, rt + 1), not_last_t),
        "bot": (at_role(rk, rt + 1), not_last_t, at_role(rk, rt - 1), not_first_t),
        "down": (at_role(rk - 1, rt), not_first_k, at_role(rk + 1, rt), not_last_k),
        "fresh": ((tm, sp + 1), fresh_out, (tm, sp - 1), fresh_far),
    }

    barrier = pltpu.get_barrier_semaphore()
    for target, sends, source, receives in links.values():
        @pl.when(receives)
        def _():
            pl.semaphore_signal(barrier, inc=1, device_id=source, device_id_type=MESH)

    def remote(link, slot, src, dst):
        return pltpu.make_async_remote_copy(
            src_ref=src, dst_ref=dst, send_sem=ssem.at[slot], recv_sem=rsem.at[slot],
            device_id=links[link][0], device_id_type=MESH,
        )

    def start(link, slot, src, dst):
        @pl.when(links[link][1])
        def _():
            remote(link, slot, src, dst).start()

    def sent(link, slot, src, dst):
        @pl.when(links[link][1])
        def _():
            remote(link, slot, src, dst).wait_send()

    def arrive(link, slot, src, dst):
        @pl.when(links[link][3])
        def _():
            remote(link, slot, src, dst).wait_recv()

    def home(slot, src, dst, op):
        @pl.when(jnp.logical_not(swapped))
        def _():
            getattr(pltpu.make_async_copy(src, dst, rsem.at[slot]), op)()

    size = levels // NC

    def part(i):
        return pl.ds(i * size, size)

    top, bottom = pl.ds(0, rows // 2), pl.ds(rows // 2, rows // 2)
    center, below, above = pl.ds(0, rows), pl.ds(rows, rows // 2), pl.ds(rows + rows // 2, rows // 2)

    def raw_flows(prefix, array, ring, span, slot):
        return (
            ("swap", slot(prefix + "C"), array.at[span], ring.at[span, center]),
            ("araw_top", slot(prefix + "T"), array.at[span, top], ring.at[span, below]),
            ("araw_bot", slot(prefix + "B"), array.at[span, bottom], ring.at[span, above]),
        )

    def raw_start(flows):
        for flow in flows:
            start(*flow)
        home(*flows[0][1:], "start")

    def raw_wait(flows):
        for flow in flows:
            arrive(*flow)
        home(*flows[0][1:], "wait")

    flows_c = raw_flows("C", coef, ring_c, pl.ds(0, 3), lambda n: SLOT[n])
    flows_l = [raw_flows("L", lam, ring_l, part(i), lambda n, i=i: SLOT[n] + i) for i in range(NC)]
    flows_x = [raw_flows("X", dx, ring_x, part(i), lambda n, i=i: SLOT[n] + i) for i in range(NC)]

    def halo_flows(prefix, ring):
        return [
            (
                ("top", SLOT[prefix + "T"] + i, ring.at[part(i), top], ring.at[part(i), below]),
                ("bot", SLOT[prefix + "B"] + i, ring.at[part(i), bottom], ring.at[part(i), above]),
            )
            for i in range(NC)
        ]

    halo_p, halo_q = halo_flows("P", ring_p), halo_flows("Q", ring_q)
    down_a = [("down", SLOT["A"] + i, a_buf.at[part(i)], a_in.at[part(i)]) for i in range(NC)]
    down_e = [("down", SLOT["E"] + i, e_buf.at[part(i)], e_in.at[part(i)]) for i in range(NC)]
    down_p = [("down", SLOT["P"] + i, ring_p.at[part(i), center], d2_in.at[part(i)]) for i in range(NC)]
    down_b = [("down", SLOT["B"] + i, b_buf.at[part(i)], b_in.at[part(i)]) for i in range(NC)]
    down_mu = ("down", SLOT["MU"], mu_buf, mu_in)
    flow_aux = ("swap", SLOT["AUX"], aux, aux_in)
    fresh_0 = ("fresh", SLOT["F0"], fresh.at[0], e_in)
    fresh_1 = ("fresh", SLOT["F1"], fresh.at[1], d2_in)
    out_l = [("swap", SLOT["OL"] + i, ol_buf.at[part(i)], out_lam.at[part(i)]) for i in range(NC)]
    out_x = [("swap", SLOT["OX"] + i, ox_buf.at[part(i)], out_dx.at[part(i)]) for i in range(NC)]
    out_o = ("swap", SLOT["OO"], oo_buf, out_obs)

    rings = (ring_l, ring_x, ring_p, ring_q, ring_c)

    @pl.when(jnp.logical_not(not_first_t))
    def _():
        for ring in rings:
            ring[:, rows + rows // 2:, :] = jnp.zeros((ring.shape[0], rows // 2, cols), F32)

    @pl.when(jnp.logical_not(not_last_t))
    def _():
        for ring in rings:
            ring[:, rows:rows + rows // 2, :] = jnp.zeros((ring.shape[0], rows // 2, cols), F32)

    @pl.when(jnp.logical_not(not_last_k))
    def _():
        a_in[...] = jnp.zeros(a_in.shape, F32)
        b_in[...] = jnp.zeros(b_in.shape, F32)

    aux[...] = jnp.zeros(aux.shape, F32)
    aux[0:1, :] = mult[...]
    aux[1:2, :] = fobs[...]
    aux[2:3, :] = ovar[...]
    aux[3:4, :] = oidx[...].astype(F32)
    aux[4:5, 0:levels] = sigma[...]

    pl.semaphore_wait(barrier, sum(link[1].astype(jnp.int32) for link in links.values()))

    raw_start(flows_c)
    start(*flow_aux)
    for i in range(NC):
        raw_start(flows_l[i])
    start(*fresh_0)
    start(*fresh_1)

    @pl.when(fresh_own)
    def _():
        pltpu.make_async_copy(fresh.at[0], e_in, rsem.at[SLOT["F0"]]).start()
        pltpu.make_async_copy(fresh.at[1], d2_in, rsem.at[SLOT["F1"]]).start()

    @pl.when(jnp.logical_not(swapped))
    def _():
        aux_in[...] = aux[...]

    arrive(*flow_aux)
    index = aux_in[3:4, :].astype(jnp.int32)
    row_of, col_of = index // cols, index % cols
    onehot[...] = jnp.where(
        lax.broadcasted_iota(jnp.int32, (levels * rows, nobs), 0) == row_of, 1.0, 0.0
    ).astype(BF16)
    mu = aux_in[0:1, :]
    var = aux_in[2:3, :]
    at_col = lax.broadcasted_iota(jnp.int32, (cols, nobs), 0) == col_of

    def spread(weights):
        high, low = halves(jnp.where(at_col, weights, 0.0))
        nt = (((1,), (1,)), ((), ()))
        total = lax.dot_general(onehot[...], high, nt, preferred_element_type=F32)
        total += lax.dot_general(onehot[...], low, nt, preferred_element_type=F32)
        ht[...] = total.reshape(ht.shape)

    def sampled(field):
        high, low = halves(field.reshape(levels * rows, cols))
        tn = (((0,), (0,)), ((), ()))
        total = lax.dot_general(high, onehot[...], tn, preferred_element_type=F32)
        total += lax.dot_general(low, onehot[...], tn, preferred_element_type=F32)
        return jnp.sum(jnp.where(at_col, total, 0.0), axis=0, keepdims=True)

    spread(mu)

    square = (levels, levels)
    lev_i = lax.broadcasted_iota(jnp.int32, square, 0)
    lev_j = lax.broadcasted_iota(jnp.int32, square, 1)
    nb = pattern.shape[0]
    wide = (
        lax.broadcasted_iota(jnp.int32, (levels, nb), 0) // LB
        == lax.broadcasted_iota(jnp.int32, (levels, nb), 1)
    ).astype(F32)
    keep = lax.dot_general(
        jnp.dot(wide, pattern[...].astype(F32), preferred_element_type=F32),
        wide, (((1,), (1,)), ((), ())), preferred_element_type=F32,
    )
    keep = jnp.maximum(keep, (lev_i // LB == lev_j // LB).astype(F32))
    eye = (lev_i == lev_j).astype(F32)
    sig_row = aux_in[4:5, 0:levels]
    sig_col = jnp.sum(eye * sig_row, axis=1, keepdims=True)
    v_high, v_low = halves(sig_col * (2.0 * eye + keep * vert[...]) * sig_row)
    deep = v3.shape[1] // 3
    pick_i = lax.broadcasted_iota(jnp.int32, (levels, 3 * deep), 0)
    pick_j = lax.broadcasted_iota(jnp.int32, (levels, 3 * deep), 1)
    first_two = jnp.logical_or(pick_j == pick_i, pick_j == pick_i + deep).astype(BF16)
    third = (pick_j == pick_i + 2 * deep).astype(BF16)
    v3[...] = (
        jnp.dot(v_high, first_two, preferred_element_type=F32)
        + jnp.dot(v_low, third, preferred_element_type=F32)
    ).astype(BF16)

    def vertical(ring, write):
        pad = jnp.zeros((deep - levels, cols), F32)
        for y in range(rows):
            def row(r):
                return ring[:, (r + 2 * rows) % (2 * rows), :]
            mid = row(y)
            smooth = 0.6 * mid + 0.1 * (
                row(y - 1) + row(y + 1) + pltpu.roll(mid, 1, 1) + pltpu.roll(mid, cols - 1, 1)
            )
            high, low = halves(jnp.concatenate([smooth, pad], axis=0))
            stack = jnp.concatenate([high, low, high], axis=0)
            write(y, jnp.dot(v3[...], stack, preferred_element_type=F32))

    def store_dl(y, value):
        dl[:, y, :] = value

    raw_wait(flows_c)
    cen[...] = 1.0 - 2.0 * ring_c[0] - 2.0 * ring_c[1] - ring_c[2]
    rid = lax.broadcasted_iota(jnp.int32, (rows, cols), 0)
    inside = jnp.where(rid < rows // 2, not_last_t.astype(F32), not_first_t.astype(F32))

    def shifted(own, other, s):
        wrap = rid < s if s > 0 else rid >= rows + s
        return jnp.where(wrap, pltpu.roll(other, s % rows, 0), pltpu.roll(own, s % rows, 0))

    def tl_tile(own, other, rs):
        near = shifted(own, other, 1) + shifted(own, other, -1)
        far = shifted(own, other, 2) + shifted(own, other, -2)
        return (
            cen[rs, :] * own + ring_c[0, rs, :] * near + ring_c[1, rs, :] * far
            + ring_c[2, rs, :] * pltpu.roll(own, 1, 1)
        )

    main, side = pl.ds(0, rows), pl.ds(rows, rows)

    def tl_model(ring, l):
        own, other = ring[l, 0:rows, :], ring[l, rows:, :]
        first, second = tl_tile(own, other, main), tl_tile(other, own, side)
        return tl_tile(first, second, main)

    def ad_tile(own, other, p, p2, r, r2, rs):
        return (
            cen[rs, :] * own + (shifted(p, p2, 1) + shifted(p, p2, -1))
            + (shifted(r, r2, 2) + shifted(r, r2, -2))
            + pltpu.roll(ring_c[2, rs, :] * own, cols - 1, 1)
        )

    def ad_model(ring, l):
        own, other = ring[l, 0:rows, :], ring[l, rows:, :]
        for step in range(2):
            p, p2 = ring_c[0, main, :] * own, ring_c[0, side, :] * other
            r, r2 = ring_c[1, main, :] * own, ring_c[1, side, :] * other
            new = ad_tile(own, other, p, p2, r, r2, main)
            if step == 0:
                other = ad_tile(other, own, p2, p, r2, r, side) * inside
            own = new
        return own

    def for_levels(i, body):
        def some(g, carry):
            for u in range(GROUP):
                body(i * size + g * GROUP + u)
            return carry
        lax.fori_loop(0, size // GROUP, some, 0)

    for i in range(NC):
        raw_wait(flows_l[i])
        raw_start(flows_x[i])

        def body(l):
            a_buf[l] = ad_model(ring_l, l)
        for_levels(i, body)
        start(*down_a[i])

    for i in range(NC):
        arrive(*down_a[i])

        def body(l):
            ring_p[l, 0:rows, :] = ring_l[l, 0:rows, :] - a_in[l] + ht[l]
        for_levels(i, body)
        for flow in halo_p[i]:
            start(*flow)
        start(*down_p[i])

    vertical(ring_l, store_dl)

    for i in range(NC):
        raw_wait(flows_x[i])

        def body(l):
            e_buf[l] = dl[l] + ring_x[l, 0:rows, :]
        for_levels(i, body)
        start(*down_e[i])

        def body(l):
            m_buf[l] = tl_model(ring_x, l)
        for_levels(i, body)

    mu_buf[...] = jnp.broadcast_to(var * mu + sampled(ring_x[:, 0:rows, :]), mu_buf.shape)
    start(*down_mu)

    arrive(*fresh_0)
    arrive(*fresh_1)

    @pl.when(fresh_own)
    def _():
        pltpu.make_async_copy(fresh.at[0], e_in, rsem.at[SLOT["F0"]]).wait()
        pltpu.make_async_copy(fresh.at[1], d2_in, rsem.at[SLOT["F1"]]).wait()

    @pl.when(jnp.logical_not(not_last_k))
    def _():
        mu_in[...] = jnp.broadcast_to(aux_in[1:2, :], mu_in.shape)
        m_buf[...] = jnp.zeros(m_buf.shape, F32)

    for i in range(NC):
        arrive(*down_e[i])

        def body(l):
            ring_q[l, 0:rows, :] = e_in[l] - m_buf[l]
        for_levels(i, body)
        for flow in halo_q[i]:
            start(*flow)

    keep_tl = not_first_k.astype(F32)
    for i in range(NC):
        for flow in halo_p[i]:
            arrive(*flow)
        arrive(*down_p[i])

        def body(l):
            n_buf[l] = d2_in[l] - keep_tl * tl_model(ring_p, l)
        for_levels(i, body)

    for i in range(NC):
        for flow in halo_q[i]:
            arrive(*flow)

        def body(l):
            b_buf[l] = ad_model(ring_q, l)
        for_levels(i, body)
        start(*down_b[i])

    vertical(ring_q, store_dl)
    for i in range(NC):
        def body(l):
            ol_buf[l] = dl[l] + n_buf[l]
        for_levels(i, body)
        start(*out_l[i])
        home(*out_l[i][1:], "start")

    arrive(*down_mu)
    mu_two = mu_in[0:1, :]
    oo_buf[...] = var * mu_two + sampled(d2_in[...])
    start(*out_o)

    @pl.when(jnp.logical_not(swapped))
    def _():
        out_obs[...] = oo_buf[...]

    spread(mu_two)
    for i in range(NC):
        arrive(*down_b[i])

        def body(l):
            ox_buf[l] = ring_q[l, 0:rows, :] - b_in[l] + ht[l]
        for_levels(i, body)
        start(*out_x[i])
        home(*out_x[i][1:], "start")

    everything = [flow_aux, fresh_0, fresh_1, down_mu, out_o, *flows_c]
    for group in (*flows_l, *flows_x, *halo_p, *halo_q):
        everything += list(group)
    everything += down_a + down_e + down_p + down_b + out_l + out_x
    for flow in everything:
        sent(*flow)
    for flow in (*out_l, *out_x):
        arrive(*flow)
        home(*flow[1:], "wait")
    arrive(*out_o)


def local(
    lam,
    obs_mult,
    dx,
    fresh_state,
    fresh_obs,
    sigma,
    obs_var,
    obs_idx,
    stencil_coef,
    vert_cov,
    block_pattern,
):
    field = dx.shape[1:]
    levels, rows, cols = field
    nobs = obs_mult.shape[1]
    ring = (levels, 2 * rows, cols)
    deep = -(-levels // 16) * 16
    anywhere, vmem = pl.BlockSpec(memory_space=pl.ANY), pl.BlockSpec(memory_space=pltpu.VMEM)
    out_lam, out_obs, out_dx = pl.pallas_call(
        kernel,
        name="saddle_slide",
        out_shape=(
            jax.ShapeDtypeStruct(field, F32),
            jax.ShapeDtypeStruct((1, nobs), F32),
            jax.ShapeDtypeStruct(field, F32),
        ),
        in_specs=[anywhere, vmem, anywhere, anywhere, vmem, vmem, vmem, vmem, anywhere, vmem, vmem],
        out_specs=(anywhere, vmem, anywhere),
        scratch_shapes=[
            *[pltpu.VMEM(ring, F32)] * 4,
            pltpu.VMEM((3, 2 * rows, cols), F32),
            pltpu.VMEM((2 * rows, cols), F32),
            *[pltpu.VMEM(field, F32)] * 13,
            pltpu.VMEM((8, nobs), F32),
            pltpu.VMEM((8, nobs), F32),
            pltpu.VMEM((8, nobs), F32),
            pltpu.VMEM((8, nobs), F32),
            pltpu.VMEM((1, nobs), F32),
            pltpu.VMEM((levels, 3 * deep), BF16),
            pltpu.VMEM((levels * rows, nobs), BF16),
            pltpu.SemaphoreType.DMA((NSEM,)),
            pltpu.SemaphoreType.DMA((NSEM,)),
        ],
        compiler_params=pltpu.CompilerParams(
            collective_id=0, has_side_effects=True, vmem_limit_bytes=48 * 2**20
        ),
        cost_estimate=pl.CostEstimate(flops=10**9, bytes_accessed=5 * 10**6, transcendentals=0),
    )(
        lam[0],
        obs_mult,
        dx[0],
        fresh_state,
        fresh_obs[None],
        sigma,
        obs_var[None],
        obs_idx[None],
        stencil_coef,
        vert_cov,
        block_pattern,
    )
    return out_lam[None], out_obs, out_dx[None]


def solution(mesh):
    in_specs = (
        P("tm", None, "space", None),
        P("tm", "space"),
        P("tm", None, "space", None),
        P(None, None, "space", None),
        P("space"),
        P("tm", None),
        P("space"),
        P("space"),
        P(None, "space", None),
        P(),
        P(),
    )
    out_specs = (P("tm", None, "space", None), P("tm", "space"), P("tm", None, "space", None))
    return jax.shard_map(local, mesh=mesh, in_specs=in_specs, out_specs=out_specs, check_vma=False)
```

```python
import jax
import jax.numpy as jnp
from jax import lax
from jax.experimental import pallas as pl
from jax.experimental.pallas import tpu as pltpu
from jax.sharding import PartitionSpec as P

MESH = pl.DeviceIdType.MESH
F32 = jnp.float32
BF16 = jnp.bfloat16
LB = 8
NC = 3
GROUP = 4
CHUNKED = ("LC", "LT", "LB", "XC", "XT", "XB", "A", "E", "P", "B", "PT", "PB", "QT", "QB", "OL", "OX", "LF", "XF")
SINGLE = ("CC", "CT", "CB", "AUX", "F0", "F1", "MU", "OO")
SLOT = {name: i * NC for i, name in enumerate(CHUNKED)}
SLOT.update({name: len(CHUNKED) * NC + i for i, name in enumerate(SINGLE)})
NSEM = len(CHUNKED) * NC + len(SINGLE)


def halves(v):
    high = v.astype(BF16)
    return high, (v - high.astype(F32)).astype(BF16)


def kernel(
    lam, mult_hbm, dx, fresh, fobs_hbm, sigma_hbm, ovar_hbm, oidx_hbm, coef, vert_hbm, pattern_hbm,
    out_lam, out_obs, out_dx,
    ring_l, ring_x, ring_p, ring_q, ring_c, cen,
    a_buf, a_in, e_buf, e_in, m_buf, n_buf, b_buf, b_in, d2_in, dl, ht, ol_buf, ox_buf,
    aux, aux_in, mu_buf, mu_in, oo_buf, v3, onehot,
    mult, fobs, sigma, ovar, oidx, vert, pattern, ssem, rsem, fsem,
):
    fetches = [
        pltpu.make_async_copy(src, dst, fsem.at[i])
        for i, (src, dst) in enumerate((
            (mult_hbm, mult), (fobs_hbm, fobs), (sigma_hbm, sigma), (ovar_hbm, ovar), (oidx_hbm, oidx),
            (vert_hbm, vert), (pattern_hbm, pattern),
        ))
    ]
    for fetch in fetches:
        fetch.start()
    levels, rows, cols = a_buf.shape
    nobs = oo_buf.shape[1]
    tms, sps = lax.axis_size("tm"), lax.axis_size("space")
    tm, sp = lax.axis_index("tm"), lax.axis_index("space")
    yl, c = lax.rem(tm, 2), lax.rem(sp, 2)
    rk, rt = tm - yl + c, sp - c + yl
    swapped = yl != c

    def at_role(k, t):
        kb, tb = lax.rem(k + 2, 2), lax.rem(t + 2, 2)
        return (k - kb + tb, t - tb + kb)

    partner = at_role(tm, sp)
    not_first_t, not_last_t = rt > 0, rt < sps - 1
    not_first_k, not_last_k = rk > 0, rk < tms - 1
    fresh_out = jnp.logical_and(tm == tms - 2, c == 0)
    fresh_far = jnp.logical_and(tm == tms - 2, c == 1)
    fresh_own = jnp.logical_and(tm == tms - 1, c == 1)
    left_top = jnp.logical_and(yl == 1, c == 0)
    left_bot = jnp.logical_and(yl == 0, c == 1)
    high_high, low_low = jnp.logical_and(yl == 1, c == 1), jnp.logical_and(yl == 0, c == 0)
    links = {
        "swap": (partner, swapped, partner, swapped),
        "araw_top": (at_role(tm, sp - 1), sp > 0, (rk, rt + 1), not_last_t),
        "araw_bot": (at_role(tm, sp + 1), sp < sps - 1, (rk, rt - 1), not_first_t),
        "top": (at_role(rk, rt - 1), not_first_t, at_role(rk, rt + 1), not_last_t),
        "bot": (at_role(rk, rt + 1), not_last_t, at_role(rk, rt - 1), not_first_t),
        "down": (at_role(rk - 1, rt), not_first_k, at_role(rk + 1, rt), not_last_k),
        "fresh": ((tm, sp + 1), fresh_out, (tm, sp - 1), fresh_far),
    }
    peers = tuple(links.values())

    def narrowed(name, sends, receives):
        target, may_send, source, may_receive = links[name]
        return (target, jnp.logical_and(may_send, sends), source, jnp.logical_and(may_receive, receives))

    links["own_top"] = narrowed("araw_top", jnp.logical_not(left_top), jnp.logical_not(high_high))
    links["own_bot"] = narrowed("araw_bot", jnp.logical_not(left_bot), jnp.logical_not(low_low))
    links["on_top"] = narrowed("top", left_bot, high_high)
    links["on_bot"] = narrowed("bot", left_top, low_low)

    barrier = pltpu.get_barrier_semaphore()
    for target, sends, source, receives in peers:
        @pl.when(receives)
        def _():
            pl.semaphore_signal(barrier, inc=1, device_id=source, device_id_type=MESH)

    def remote(link, slot, src, dst):
        return pltpu.make_async_remote_copy(
            src_ref=src, dst_ref=dst, send_sem=ssem.at[slot], recv_sem=rsem.at[slot],
            device_id=links[link][0], device_id_type=MESH,
        )

    def start(link, slot, src, dst):
        @pl.when(links[link][1])
        def _():
            remote(link, slot, src, dst).start()

    def sent(link, slot, src, dst):
        @pl.when(links[link][1])
        def _():
            remote(link, slot, src, dst).wait_send()

    def arrive(link, slot, src, dst):
        @pl.when(links[link][3])
        def _():
            remote(link, slot, src, dst).wait_recv()

    def home(slot, src, dst, op):
        @pl.when(jnp.logical_not(swapped))
        def _():
            getattr(pltpu.make_async_copy(src, dst, rsem.at[slot]), op)()

    size = levels // NC

    def part(i):
        return pl.ds(i * size, size)

    top, bottom = pl.ds(0, rows // 2), pl.ds(rows // 2, rows // 2)
    center, below, above = pl.ds(0, rows), pl.ds(rows, rows // 2), pl.ds(rows + rows // 2, rows // 2)

    def raw_flows(prefix, array, ring, span, links, i=0):
        return (
            ("swap", SLOT[prefix + "C"] + i, array.at[span], ring.at[span, center]),
            (links + "top", SLOT[prefix + "T"] + i, array.at[span, top], ring.at[span, below]),
            (links + "bot", SLOT[prefix + "B"] + i, array.at[span, bottom], ring.at[span, above]),
        )

    def raw_start(flows):
        for flow in flows:
            start(*flow)
        home(*flows[0][1:], "start")

    def raw_center(flows):
        arrive(*flows[0])
        home(*flows[0][1:], "wait")

    def raw_edges(flows):
        for flow in flows[1:]:
            arrive(*flow)

    def on_flows(prefix, ring):
        return [
            (
                ("on_top", SLOT[prefix + "F"] + i, ring.at[part(i), top], ring.at[part(i), below]),
                ("on_bot", SLOT[prefix + "F"] + i, ring.at[part(i), bottom], ring.at[part(i), above]),
            )
            for i in range(NC)
        ]

    flows_c = raw_flows("C", coef, ring_c, pl.ds(0, 3), "araw_")
    flows_l = [raw_flows("L", lam, ring_l, part(i), "own_", i) for i in range(NC)]
    flows_x = [raw_flows("X", dx, ring_x, part(i), "own_", i) for i in range(NC)]
    on_l, on_x = on_flows("L", ring_l), on_flows("X", ring_x)

    def halo_flows(prefix, ring):
        return [
            (
                ("top", SLOT[prefix + "T"] + i, ring.at[part(i), top], ring.at[part(i), below]),
                ("bot", SLOT[prefix + "B"] + i, ring.at[part(i), bottom], ring.at[part(i), above]),
            )
            for i in range(NC)
        ]

    halo_p, halo_q = halo_flows("P", ring_p), halo_flows("Q", ring_q)
    down_a = [("down", SLOT["A"] + i, a_buf.at[part(i)], a_in.at[part(i)]) for i in range(NC)]
    down_e = [("down", SLOT["E"] + i, e_buf.at[part(i)], e_in.at[part(i)]) for i in range(NC)]
    down_p = [("down", SLOT["P"] + i, ring_p.at[part(i), center], d2_in.at[part(i)]) for i in range(NC)]
    down_b = [("down", SLOT["B"] + i, b_buf.at[part(i)], b_in.at[part(i)]) for i in range(NC)]
    down_mu = ("down", SLOT["MU"], mu_buf, mu_in)
    flow_aux = ("swap", SLOT["AUX"], aux, aux_in)
    fresh_0 = ("fresh", SLOT["F0"], fresh.at[0], e_in)
    fresh_1 = ("fresh", SLOT["F1"], fresh.at[1], d2_in)
    out_l = [("swap", SLOT["OL"] + i, ol_buf.at[part(i)], out_lam.at[part(i)]) for i in range(NC)]
    out_x = [("swap", SLOT["OX"] + i, ox_buf.at[part(i)], out_dx.at[part(i)]) for i in range(NC)]
    out_o = ("swap", SLOT["OO"], oo_buf, out_obs)

    aux[...] = jnp.zeros(aux.shape, F32)
    for fetch in fetches:
        fetch.wait()
    aux[0:1, :] = mult[...]
    aux[1:2, :] = fobs[...]
    aux[2:3, :] = ovar[...]
    aux[3:4, :] = oidx[...].astype(F32)
    aux[4:5, 0:levels] = sigma[...]

    pl.semaphore_wait(barrier, sum(peer[1].astype(jnp.int32) for peer in peers))

    raw_start(flows_c)
    start(*flow_aux)
    for i in range(NC):
        raw_start(flows_l[i])

    rings = (ring_l, ring_x, ring_p, ring_q, ring_c)

    @pl.when(jnp.logical_not(not_first_t))
    def _():
        for ring in rings:
            ring[:, rows + rows // 2:, :] = jnp.zeros((ring.shape[0], rows // 2, cols), F32)

    @pl.when(jnp.logical_not(not_last_t))
    def _():
        for ring in rings:
            ring[:, rows:rows + rows // 2, :] = jnp.zeros((ring.shape[0], rows // 2, cols), F32)

    @pl.when(jnp.logical_not(not_last_k))
    def _():
        a_in[...] = jnp.zeros(a_in.shape, F32)
        b_in[...] = jnp.zeros(b_in.shape, F32)

    start(*fresh_0)
    start(*fresh_1)

    @pl.when(fresh_own)
    def _():
        pltpu.make_async_copy(fresh.at[0], e_in, rsem.at[SLOT["F0"]]).start()
        pltpu.make_async_copy(fresh.at[1], d2_in, rsem.at[SLOT["F1"]]).start()

    @pl.when(jnp.logical_not(swapped))
    def _():
        aux_in[...] = aux[...]

    arrive(*flow_aux)
    index = aux_in[3:4, :].astype(jnp.int32)
    row_of, col_of = index // cols, index % cols
    onehot[...] = jnp.where(
        lax.broadcasted_iota(jnp.int32, (levels * rows, nobs), 0) == row_of, 1.0, 0.0
    ).astype(BF16)
    mu = aux_in[0:1, :]
    var = aux_in[2:3, :]
    at_col = lax.broadcasted_iota(jnp.int32, (cols, nobs), 0) == col_of

    def spread(weights):
        high, low = halves(jnp.where(at_col, weights, 0.0))
        nt = (((1,), (1,)), ((), ()))
        total = lax.dot_general(onehot[...], high, nt, preferred_element_type=F32)
        total += lax.dot_general(onehot[...], low, nt, preferred_element_type=F32)
        ht[...] = total.reshape(ht.shape)

    def sampled(field):
        high, low = halves(field.reshape(levels * rows, cols))
        tn = (((0,), (0,)), ((), ()))
        total = lax.dot_general(high, onehot[...], tn, preferred_element_type=F32)
        total += lax.dot_general(low, onehot[...], tn, preferred_element_type=F32)
        return jnp.sum(jnp.where(at_col, total, 0.0), axis=0, keepdims=True)

    spread(mu)

    square = (levels, levels)
    lev_i = lax.broadcasted_iota(jnp.int32, square, 0)
    lev_j = lax.broadcasted_iota(jnp.int32, square, 1)
    nb = pattern.shape[0]
    wide = (
        lax.broadcasted_iota(jnp.int32, (levels, nb), 0) // LB
        == lax.broadcasted_iota(jnp.int32, (levels, nb), 1)
    ).astype(F32)
    keep = lax.dot_general(
        jnp.dot(wide, pattern[...].astype(F32), preferred_element_type=F32),
        wide, (((1,), (1,)), ((), ())), preferred_element_type=F32,
    )
    keep = jnp.maximum(keep, (lev_i // LB == lev_j // LB).astype(F32))
    eye = (lev_i == lev_j).astype(F32)
    sig_row = aux_in[4:5, 0:levels]
    sig_col = jnp.sum(eye * sig_row, axis=1, keepdims=True)
    v_high, v_low = halves(sig_col * (2.0 * eye + keep * vert[...]) * sig_row)
    deep = v3.shape[1] // 3
    pick_i = lax.broadcasted_iota(jnp.int32, (levels, 3 * deep), 0)
    pick_j = lax.broadcasted_iota(jnp.int32, (levels, 3 * deep), 1)
    first_two = jnp.logical_or(pick_j == pick_i, pick_j == pick_i + deep).astype(BF16)
    third = (pick_j == pick_i + 2 * deep).astype(BF16)
    v3[...] = (
        jnp.dot(v_high, first_two, preferred_element_type=F32)
        + jnp.dot(v_low, third, preferred_element_type=F32)
    ).astype(BF16)

    def vertical(ring, write):
        pad = jnp.zeros((deep - levels, cols), F32)
        before, mid = ring[:, 2 * rows - 1, :], ring[:, 0, :]
        for y in range(rows):
            after = ring[:, y + 1, :]
            smooth = 0.6 * mid + 0.1 * (
                before + after + pltpu.roll(mid, 1, 1) + pltpu.roll(mid, cols - 1, 1)
            )
            before, mid = mid, after
            high, low = halves(jnp.concatenate([smooth, pad], axis=0))
            stack = jnp.concatenate([high, low, high], axis=0)
            write(y, jnp.dot(v3[...], stack, preferred_element_type=F32))

    def store_dl(y, value):
        dl[:, y, :] = value

    raw_center(flows_c)
    raw_edges(flows_c)
    cen[...] = 1.0 - 2.0 * ring_c[0] - 2.0 * ring_c[1] - ring_c[2]
    rid = lax.broadcasted_iota(jnp.int32, (rows, cols), 0)
    inside = jnp.where(rid < rows // 2, not_last_t.astype(F32), not_first_t.astype(F32))

    def shifted(own, other, s):
        wrap = rid >= rows - s if s > 0 else rid < -s
        return pltpu.roll(jnp.where(wrap, other, own), s % rows, 0)

    def tl_tile(own, other, rs):
        near = shifted(own, other, 1) + shifted(own, other, -1)
        far = shifted(own, other, 2) + shifted(own, other, -2)
        return (
            cen[rs, :] * own + ring_c[0, rs, :] * near + ring_c[1, rs, :] * far
            + ring_c[2, rs, :] * pltpu.roll(own, 1, 1)
        )

    main, side = pl.ds(0, rows), pl.ds(rows, rows)

    def tl_model(ring, l):
        own, other = ring[l, 0:rows, :], ring[l, rows:, :]
        first, second = tl_tile(own, other, main), tl_tile(other, own, side)
        return tl_tile(first, second, main)

    def ad_tile(own, other, p, p2, r, r2, rs):
        return (
            cen[rs, :] * own + (shifted(p, p2, 1) + shifted(p, p2, -1))
            + (shifted(r, r2, 2) + shifted(r, r2, -2))
            + pltpu.roll(ring_c[2, rs, :] * own, cols - 1, 1)
        )

    def ad_model(ring, l):
        own, other = ring[l, 0:rows, :], ring[l, rows:, :]
        for step in range(2):
            p, p2 = ring_c[0, main, :] * own, ring_c[0, side, :] * other
            r, r2 = ring_c[1, main, :] * own, ring_c[1, side, :] * other
            new = ad_tile(own, other, p, p2, r, r2, main)
            if step == 0:
                other = ad_tile(other, own, p2, p, r2, r, side) * inside
            own = new
        return own

    def for_levels(i, body):
        def some(g, carry):
            for u in range(GROUP):
                body(i * size + g * GROUP + u)
            return carry
        lax.fori_loop(0, size // GROUP, some, 0)

    def do_l(i):
        raw_center(flows_l[i])
        for flow in on_l[i]:
            start(*flow)
        raw_start(flows_x[i])
        raw_edges(flows_l[i])
        for flow in on_l[i]:
            arrive(*flow)

    def do_a(i):
        def body(l):
            a_buf[l] = ad_model(ring_l, l)
        for_levels(i, body)
        start(*down_a[i])

    def do_e(i):
        raw_center(flows_x[i])
        for flow in on_x[i]:
            start(*flow)

        def body(l):
            e_buf[l] = dl[l] + ring_x[l, 0:rows, :]
        for_levels(i, body)
        start(*down_e[i])

    def do_p(i):
        arrive(*down_a[i])

        def body(l):
            ring_p[l, 0:rows, :] = ring_l[l, 0:rows, :] - a_in[l] + ht[l]
        for_levels(i, body)
        for flow in halo_p[i]:
            start(*flow)

    def do_m(i):
        raw_edges(flows_x[i])
        for flow in on_x[i]:
            arrive(*flow)

        def body(l):
            m_buf[l] = jnp.where(not_last_k, tl_model(ring_x, l), 0.0)
        for_levels(i, body)

    def do_q(i):
        arrive(*down_e[i])

        def body(l):
            ring_q[l, 0:rows, :] = e_in[l] - m_buf[l]
        for_levels(i, body)
        for flow in halo_q[i]:
            start(*flow)

    def do_n(i):
        for flow in halo_p[i]:
            arrive(*flow)

        def body(l):
            n_buf[l] = jnp.where(not_first_k, tl_model(ring_p, l), 0.0)
        for_levels(i, body)

    def do_b(i):
        for flow in halo_q[i]:
            arrive(*flow)

        def body(l):
            b_buf[l] = ad_model(ring_q, l)
        for_levels(i, body)
        start(*down_b[i])

    def do_ol(i):
        arrive(*down_p[i])

        def body(l):
            ol_buf[l] = dl[l] + (d2_in[l] - n_buf[l])
        for_levels(i, body)
        start(*out_l[i])
        home(*out_l[i][1:], "start")

    def do_ox(i):
        arrive(*down_b[i])

        def body(l):
            ox_buf[l] = ring_q[l, 0:rows, :] - b_in[l] + ht[l]
        for_levels(i, body)
        start(*out_x[i])
        home(*out_x[i][1:], "start")

    for i in range(NC):
        do_l(i)
        do_a(i)
    vertical(ring_l, store_dl)
    do_p(0)
    for i in range(NC):
        do_e(i)
        if i + 1 < NC:
            do_p(i + 1)
        do_m(i)
        if i == 0:
            arrive(*fresh_0)
            arrive(*fresh_1)

            @pl.when(fresh_own)
            def _():
                pltpu.make_async_copy(fresh.at[0], e_in, rsem.at[SLOT["F0"]]).wait()
                pltpu.make_async_copy(fresh.at[1], d2_in, rsem.at[SLOT["F1"]]).wait()
        else:
            do_q(i - 1)
    for i in range(NC):
        start(*down_p[i])
    mu_buf[...] = jnp.broadcast_to(var * mu + sampled(ring_x[:, 0:rows, :]), mu_buf.shape)
    start(*down_mu)
    do_q(NC - 1)

    @pl.when(jnp.logical_not(not_last_k))
    def _():
        mu_in[...] = jnp.broadcast_to(aux_in[1:2, :], mu_in.shape)

    for i in range(NC):
        do_n(i)
        if i == NC - 1:
            arrive(*down_mu)
            mu_two = mu_in[0:1, :]
            spread(mu_two)
        do_b(i)
    do_ox(0)
    vertical(ring_q, store_dl)
    for i in range(NC):
        do_ol(i)
    oo_buf[...] = var * mu_two + sampled(d2_in[...])
    start(*out_o)

    @pl.when(jnp.logical_not(swapped))
    def _():
        out_obs[...] = oo_buf[...]

    for i in range(1, NC):
        do_ox(i)

    everything = [flow_aux, fresh_0, fresh_1, down_mu, out_o, *flows_c]
    for group in (*flows_l, *flows_x, *on_l, *on_x, *halo_p, *halo_q):
        everything += list(group)
    everything += down_a + down_e + down_p + down_b + out_l + out_x
    for flow in everything:
        sent(*flow)
    for flow in (*out_l, *out_x):
        arrive(*flow)
        home(*flow[1:], "wait")
    arrive(*out_o)


def hand_over(*refs):
    sources, targets, stops, sems = refs[:3], refs[3:6], refs[6:9], refs[9]
    inward, outward = [], []
    for source, target, stop in zip(sources, targets, stops):
        pieces = 3 if len(source.shape) == 3 else 1
        step = source.shape[0] // pieces
        for i in range(pieces):
            span, n = pl.ds(i * step, step), len(inward)
            inward.append(pltpu.make_async_copy(source.at[span], stop.at[span], sems.at[0, n]))
            outward.append(pltpu.make_async_copy(stop.at[span], target.at[span], sems.at[1, n]))
    for copy in inward:
        copy.start()
    for first, second in zip(inward, outward):
        first.wait()
        second.start()
    for copy in outward:
        copy.wait()


def local(
    lam,
    obs_mult,
    dx,
    fresh_state,
    fresh_obs,
    sigma,
    obs_var,
    obs_idx,
    stencil_coef,
    vert_cov,
    block_pattern,
):
    field = dx.shape[1:]
    levels, rows, cols = field
    nobs = obs_mult.shape[1]
    ring = (levels, 2 * rows, cols)
    deep = -(-levels // 16) * 16
    anywhere, vmem = pl.BlockSpec(memory_space=pl.ANY), pl.BlockSpec(memory_space=pltpu.VMEM)
    out_lam, out_obs, out_dx = pl.pallas_call(
        kernel,
        name="saddle_slide",
        out_shape=(
            jax.ShapeDtypeStruct(field, F32),
            jax.ShapeDtypeStruct((1, nobs), F32),
            jax.ShapeDtypeStruct(field, F32),
        ),
        in_specs=[anywhere] * 11,
        out_specs=(anywhere, vmem, anywhere),
        scratch_shapes=[
            *[pltpu.VMEM(ring, F32)] * 4,
            pltpu.VMEM((3, 2 * rows, cols), F32),
            pltpu.VMEM((2 * rows, cols), F32),
            *[pltpu.VMEM(field, F32)] * 13,
            pltpu.VMEM((8, nobs), F32),
            pltpu.VMEM((8, nobs), F32),
            pltpu.VMEM((8, nobs), F32),
            pltpu.VMEM((8, nobs), F32),
            pltpu.VMEM((1, nobs), F32),
            pltpu.VMEM((levels, 3 * deep), BF16),
            pltpu.VMEM((levels * rows, nobs), BF16),
            pltpu.VMEM((1, nobs), F32),
            pltpu.VMEM((1, nobs), F32),
            pltpu.VMEM((1, levels), F32),
            pltpu.VMEM((1, nobs), F32),
            pltpu.VMEM((1, nobs), jnp.int32),
            pltpu.VMEM(vert_cov.shape, F32),
            pltpu.VMEM(block_pattern.shape, jnp.int32),
            pltpu.SemaphoreType.DMA((NSEM,)),
            pltpu.SemaphoreType.DMA((NSEM,)),
            pltpu.SemaphoreType.DMA((7,)),
        ],
        compiler_params=pltpu.CompilerParams(
            collective_id=0, has_side_effects=True, vmem_limit_bytes=63 * 2**20
        ),
        cost_estimate=pl.CostEstimate(flops=10**9, bytes_accessed=5 * 10**6, transcendentals=0),
    )(
        lam[0],
        obs_mult,
        dx[0],
        fresh_state,
        fresh_obs[None],
        sigma,
        obs_var[None],
        obs_idx[None],
        stencil_coef,
        vert_cov,
        block_pattern,
    )
    results = (out_lam, out_obs, out_dx)
    out_lam, out_obs, out_dx = pl.pallas_call(
        hand_over,
        name="hand_over",
        out_shape=tuple(jax.ShapeDtypeStruct(r.shape, r.dtype) for r in results),
        in_specs=[anywhere] * 3,
        out_specs=(anywhere,) * 3,
        scratch_shapes=[
            *[pltpu.VMEM(r.shape, r.dtype) for r in results],
            pltpu.SemaphoreType.DMA((2, 7)),
        ],
        compiler_params=pltpu.CompilerParams(vmem_limit_bytes=63 * 2**20),
    )(*results)
    return out_lam[None], out_obs, out_dx[None]


def solution(mesh):
    in_specs = (
        P("tm", None, "space", None),
        P("tm", "space"),
        P("tm", None, "space", None),
        P(None, None, "space", None),
        P("space"),
        P("tm", None),
        P("space"),
        P("space"),
        P(None, "space", None),
        P(),
        P(),
    )
    out_specs = (P("tm", None, "space", None), P("tm", "space"), P("tm", None, "space", None))
    return jax.shard_map(local, mesh=mesh, in_specs=in_specs, out_specs=out_specs, check_vma=False)
```

```python
import jax
import jax.numpy as jnp
from jax import lax
from jax.experimental import pallas as pl
from jax.experimental.pallas import tpu as pltpu
from jax.sharding import PartitionSpec as P

MESH = pl.DeviceIdType.MESH
F32 = jnp.float32
BF16 = jnp.bfloat16
LB = 8
NC = 3
GROUP = 8
CHUNKED = ("LC", "LT", "LB", "XC", "XT", "XB", "A", "E", "P", "B", "PT", "PB", "QT", "QB", "OL", "OX", "LF", "XF")
SINGLE = ("CC", "CT", "CB", "AUX", "F0", "F1", "MU", "OO")
SLOT = {name: i * NC for i, name in enumerate(CHUNKED)}
SLOT.update({name: len(CHUNKED) * NC + i for i, name in enumerate(SINGLE)})
NSEM = len(CHUNKED) * NC + len(SINGLE)


def halves(v):
    high = v.astype(BF16)
    return high, (v - high.astype(F32)).astype(BF16)


def kernel(
    lam, mult_hbm, dx, fresh, fobs_hbm, sigma_hbm, ovar_hbm, oidx_hbm, coef, vert_hbm, pattern_hbm,
    out_lam, out_obs, out_dx,
    ring_l, ring_x, ring_p, ring_q, ring_c, cen,
    a_buf, a_in, e_buf, e_in, m_buf, n_buf, b_buf, b_in, d2_in, dl, ht, ol_buf, ox_buf,
    aux, aux_in, mu_buf, mu_in, oo_buf, v3, onehot,
    mult, fobs, sigma, ovar, oidx, vert, pattern, ssem, rsem, fsem,
):
    fetches = [
        pltpu.make_async_copy(src, dst, fsem.at[i])
        for i, (src, dst) in enumerate((
            (mult_hbm, mult), (fobs_hbm, fobs), (sigma_hbm, sigma), (ovar_hbm, ovar), (oidx_hbm, oidx),
            (vert_hbm, vert), (pattern_hbm, pattern),
        ))
    ]
    for fetch in fetches:
        fetch.start()
    levels, rows, cols = a_buf.shape
    nobs = oo_buf.shape[1]
    tms, sps = lax.axis_size("tm"), lax.axis_size("space")
    tm, sp = lax.axis_index("tm"), lax.axis_index("space")
    yl, c = lax.rem(tm, 2), lax.rem(sp, 2)
    rk, rt = tm - yl + c, sp - c + yl
    swapped = yl != c

    def at_role(k, t):
        kb, tb = lax.rem(k + 2, 2), lax.rem(t + 2, 2)
        return (k - kb + tb, t - tb + kb)

    partner = at_role(tm, sp)
    not_first_t, not_last_t = rt > 0, rt < sps - 1
    not_first_k, not_last_k = rk > 0, rk < tms - 1
    fresh_out = jnp.logical_and(tm == tms - 2, c == 0)
    fresh_far = jnp.logical_and(tm == tms - 2, c == 1)
    fresh_own = jnp.logical_and(tm == tms - 1, c == 1)
    left_top = jnp.logical_and(yl == 1, c == 0)
    left_bot = jnp.logical_and(yl == 0, c == 1)
    high_high, low_low = jnp.logical_and(yl == 1, c == 1), jnp.logical_and(yl == 0, c == 0)
    links = {
        "swap": (partner, swapped, partner, swapped),
        "araw_top": (at_role(tm, sp - 1), sp > 0, (rk, rt + 1), not_last_t),
        "araw_bot": (at_role(tm, sp + 1), sp < sps - 1, (rk, rt - 1), not_first_t),
        "top": (at_role(rk, rt - 1), not_first_t, at_role(rk, rt + 1), not_last_t),
        "bot": (at_role(rk, rt + 1), not_last_t, at_role(rk, rt - 1), not_first_t),
        "down": (at_role(rk - 1, rt), not_first_k, at_role(rk + 1, rt), not_last_k),
        "fresh": ((tm, sp + 1), fresh_out, (tm, sp - 1), fresh_far),
    }
    peers = tuple(links.values())

    def narrowed(name, sends, receives):
        target, may_send, source, may_receive = links[name]
        return (target, jnp.logical_and(may_send, sends), source, jnp.logical_and(may_receive, receives))

    links["own_top"] = narrowed("araw_top", jnp.logical_not(left_top), jnp.logical_not(high_high))
    links["own_bot"] = narrowed("araw_bot", jnp.logical_not(left_bot), jnp.logical_not(low_low))
    links["on_top"] = narrowed("top", left_bot, high_high)
    links["on_bot"] = narrowed("bot", left_top, low_low)

    barrier = pltpu.get_barrier_semaphore()
    for target, sends, source, receives in peers:
        @pl.when(receives)
        def _():
            pl.semaphore_signal(barrier, inc=1, device_id=source, device_id_type=MESH)

    def remote(link, slot, src, dst):
        return pltpu.make_async_remote_copy(
            src_ref=src, dst_ref=dst, send_sem=ssem.at[slot], recv_sem=rsem.at[slot],
            device_id=links[link][0], device_id_type=MESH,
        )

    def start(link, slot, src, dst):
        @pl.when(links[link][1])
        def _():
            remote(link, slot, src, dst).start()

    def sent(link, slot, src, dst):
        @pl.when(links[link][1])
        def _():
            remote(link, slot, src, dst).wait_send()

    def arrive(link, slot, src, dst):
        @pl.when(links[link][3])
        def _():
            remote(link, slot, src, dst).wait_recv()

    def home(slot, src, dst, op):
        @pl.when(jnp.logical_not(swapped))
        def _():
            getattr(pltpu.make_async_copy(src, dst, rsem.at[slot]), op)()

    size = levels // NC

    def part(i):
        return pl.ds(i * size, size)

    top, bottom = pl.ds(0, rows // 2), pl.ds(rows // 2, rows // 2)
    center, below, above = pl.ds(0, rows), pl.ds(rows, rows // 2), pl.ds(rows + rows // 2, rows // 2)

    def raw_flows(prefix, array, ring, span, links, i=0):
        return (
            ("swap", SLOT[prefix + "C"] + i, array.at[span], ring.at[span, center]),
            (links + "top", SLOT[prefix + "T"] + i, array.at[span, top], ring.at[span, below]),
            (links + "bot", SLOT[prefix + "B"] + i, array.at[span, bottom], ring.at[span, above]),
        )

    def start_center(flows):
        start(*flows[0])
        home(*flows[0][1:], "start")

    def start_edges(flows):
        for flow in flows[1:]:
            start(*flow)

    def raw_start(flows):
        start_center(flows)
        start_edges(flows)

    def raw_center(flows):
        arrive(*flows[0])
        home(*flows[0][1:], "wait")

    def raw_edges(flows):
        for flow in flows[1:]:
            arrive(*flow)

    def on_flows(prefix, ring):
        return [
            (
                ("on_top", SLOT[prefix + "F"] + i, ring.at[part(i), top], ring.at[part(i), below]),
                ("on_bot", SLOT[prefix + "F"] + i, ring.at[part(i), bottom], ring.at[part(i), above]),
            )
            for i in range(NC)
        ]

    flows_c = raw_flows("C", coef, ring_c, pl.ds(0, 3), "araw_")
    flows_l = [raw_flows("L", lam, ring_l, part(i), "own_", i) for i in range(NC)]
    flows_x = [raw_flows("X", dx, ring_x, part(i), "own_", i) for i in range(NC)]
    on_l, on_x = on_flows("L", ring_l), on_flows("X", ring_x)

    def halo_flows(prefix, ring):
        return [
            (
                ("top", SLOT[prefix + "T"] + i, ring.at[part(i), top], ring.at[part(i), below]),
                ("bot", SLOT[prefix + "B"] + i, ring.at[part(i), bottom], ring.at[part(i), above]),
            )
            for i in range(NC)
        ]

    halo_p, halo_q = halo_flows("P", ring_p), halo_flows("Q", ring_q)
    down_a = [("down", SLOT["A"] + i, a_buf.at[part(i)], a_in.at[part(i)]) for i in range(NC)]
    down_e = [("down", SLOT["E"] + i, e_buf.at[part(i)], e_in.at[part(i)]) for i in range(NC)]
    down_p = [("down", SLOT["P"] + i, ring_p.at[part(i), center], d2_in.at[part(i)]) for i in range(NC)]
    down_b = [("down", SLOT["B"] + i, b_buf.at[part(i)], b_in.at[part(i)]) for i in range(NC)]
    down_mu = ("down", SLOT["MU"], mu_buf, mu_in)
    flow_aux = ("swap", SLOT["AUX"], aux, aux_in)
    fresh_0 = ("fresh", SLOT["F0"], fresh.at[0], e_in)
    fresh_1 = ("fresh", SLOT["F1"], fresh.at[1], d2_in)
    out_l = [("swap", SLOT["OL"] + i, ol_buf.at[part(i)], out_lam.at[part(i)]) for i in range(NC)]
    out_x = [("swap", SLOT["OX"] + i, ox_buf.at[part(i)], out_dx.at[part(i)]) for i in range(NC)]
    out_o = ("swap", SLOT["OO"], oo_buf, out_obs)

    aux[...] = jnp.zeros(aux.shape, F32)
    for fetch in fetches:
        fetch.wait()
    aux[0:1, :] = mult[...]
    aux[1:2, :] = fobs[...]
    aux[2:3, :] = ovar[...]
    aux[3:4, :] = oidx[...].astype(F32)
    aux[4:5, 0:levels] = sigma[...]

    pl.semaphore_wait(barrier, sum(peer[1].astype(jnp.int32) for peer in peers))

    raw_start(flows_c)
    start(*flow_aux)
    for i in range(NC):
        raw_start(flows_l[i])

    rings = (ring_l, ring_x, ring_p, ring_q, ring_c)

    @pl.when(jnp.logical_not(not_first_t))
    def _():
        for ring in rings:
            ring[:, rows + rows // 2:, :] = jnp.zeros((ring.shape[0], rows // 2, cols), F32)

    @pl.when(jnp.logical_not(not_last_t))
    def _():
        for ring in rings:
            ring[:, rows:rows + rows // 2, :] = jnp.zeros((ring.shape[0], rows // 2, cols), F32)

    @pl.when(jnp.logical_not(not_last_k))
    def _():
        a_in[...] = jnp.zeros(a_in.shape, F32)
        b_in[...] = jnp.zeros(b_in.shape, F32)

    start(*fresh_0)
    start(*fresh_1)

    @pl.when(fresh_own)
    def _():
        pltpu.make_async_copy(fresh.at[0], e_in, rsem.at[SLOT["F0"]]).start()
        pltpu.make_async_copy(fresh.at[1], d2_in, rsem.at[SLOT["F1"]]).start()

    @pl.when(jnp.logical_not(swapped))
    def _():
        aux_in[...] = aux[...]

    arrive(*flow_aux)
    index = aux_in[3:4, :].astype(jnp.int32)
    row_of, col_of = index // cols, index % cols
    onehot[...] = jnp.where(
        lax.broadcasted_iota(jnp.int32, (levels * rows, nobs), 0) == row_of, 1.0, 0.0
    ).astype(BF16)
    mu = aux_in[0:1, :]
    var = aux_in[2:3, :]
    at_col = lax.broadcasted_iota(jnp.int32, (cols, nobs), 0) == col_of

    def spread(weights):
        high, low = halves(jnp.where(at_col, weights, 0.0))
        nt = (((1,), (1,)), ((), ()))
        total = lax.dot_general(onehot[...], high, nt, preferred_element_type=F32)
        total += lax.dot_general(onehot[...], low, nt, preferred_element_type=F32)
        ht[...] = total.reshape(ht.shape)

    def sampled(field):
        high, low = halves(field.reshape(levels * rows, cols))
        tn = (((0,), (0,)), ((), ()))
        total = lax.dot_general(high, onehot[...], tn, preferred_element_type=F32)
        total += lax.dot_general(low, onehot[...], tn, preferred_element_type=F32)
        return jnp.sum(jnp.where(at_col, total, 0.0), axis=0, keepdims=True)

    spread(mu)

    square = (levels, levels)
    lev_i = lax.broadcasted_iota(jnp.int32, square, 0)
    lev_j = lax.broadcasted_iota(jnp.int32, square, 1)
    nb = pattern.shape[0]
    wide = (
        lax.broadcasted_iota(jnp.int32, (levels, nb), 0) // LB
        == lax.broadcasted_iota(jnp.int32, (levels, nb), 1)
    ).astype(F32)
    keep = lax.dot_general(
        jnp.dot(wide, pattern[...].astype(F32), preferred_element_type=F32),
        wide, (((1,), (1,)), ((), ())), preferred_element_type=F32,
    )
    keep = jnp.maximum(keep, (lev_i // LB == lev_j // LB).astype(F32))
    eye = (lev_i == lev_j).astype(F32)
    sig_row = aux_in[4:5, 0:levels]
    sig_col = jnp.sum(eye * sig_row, axis=1, keepdims=True)
    v_high, v_low = halves(sig_col * (2.0 * eye + keep * vert[...]) * sig_row)
    deep = v3.shape[1] // 3
    pick_i = lax.broadcasted_iota(jnp.int32, (levels, 3 * deep), 0)
    pick_j = lax.broadcasted_iota(jnp.int32, (levels, 3 * deep), 1)
    first_two = jnp.logical_or(pick_j == pick_i, pick_j == pick_i + deep).astype(BF16)
    third = (pick_j == pick_i + 2 * deep).astype(BF16)
    v3[...] = (
        jnp.dot(v_high, first_two, preferred_element_type=F32)
        + jnp.dot(v_low, third, preferred_element_type=F32)
    ).astype(BF16)

    def vertical(ring, write):
        pad = jnp.zeros((deep - levels, cols), F32)
        before, mid = ring[:, 2 * rows - 1, :], ring[:, 0, :]
        for y in range(rows):
            after = ring[:, y + 1, :]
            smooth = 0.6 * mid + 0.1 * (
                before + after + pltpu.roll(mid, 1, 1) + pltpu.roll(mid, cols - 1, 1)
            )
            before, mid = mid, after
            high, low = halves(jnp.concatenate([smooth, pad], axis=0))
            stack = jnp.concatenate([high, low, high], axis=0)
            write(y, jnp.dot(v3[...], stack, preferred_element_type=F32))

    def store_dl(y, value):
        dl[:, y, :] = value

    raw_center(flows_c)
    raw_edges(flows_c)
    cen[...] = 1.0 - 2.0 * ring_c[0] - 2.0 * ring_c[1] - ring_c[2]
    rid = lax.broadcasted_iota(jnp.int32, (rows, cols), 0)
    inside = jnp.where(rid < rows // 2, not_last_t.astype(F32), not_first_t.astype(F32))

    def shifted(own, other, s):
        wrap = rid >= rows - s if s > 0 else rid < -s
        return pltpu.roll(jnp.where(wrap, other, own), s % rows, 0)

    def tl_tile(own, other, rs):
        near = shifted(own, other, 1) + shifted(own, other, -1)
        far = shifted(own, other, 2) + shifted(own, other, -2)
        return (
            cen[rs, :] * own + ring_c[0, rs, :] * near + ring_c[1, rs, :] * far
            + ring_c[2, rs, :] * pltpu.roll(own, 1, 1)
        )

    main, side = pl.ds(0, rows), pl.ds(rows, rows)

    def tl_model(ring, l):
        own, other = ring[l, 0:rows, :], ring[l, rows:, :]
        first, second = tl_tile(own, other, main), tl_tile(other, own, side)
        return tl_tile(first, second, main)

    def ad_tile(own, other, p, p2, r, r2, rs):
        return (
            cen[rs, :] * own + (shifted(p, p2, 1) + shifted(p, p2, -1))
            + (shifted(r, r2, 2) + shifted(r, r2, -2))
            + pltpu.roll(ring_c[2, rs, :] * own, cols - 1, 1)
        )

    def ad_model(ring, l):
        own, other = ring[l, 0:rows, :], ring[l, rows:, :]
        for step in range(2):
            p, p2 = ring_c[0, main, :] * own, ring_c[0, side, :] * other
            r, r2 = ring_c[1, main, :] * own, ring_c[1, side, :] * other
            new = ad_tile(own, other, p, p2, r, r2, main)
            if step == 0:
                other = ad_tile(other, own, p2, p, r2, r, side) * inside
            own = new
        return own

    def for_levels(i, body):
        def some(g, carry):
            for u in range(GROUP):
                body(i * size + g * GROUP + u)
            return carry
        lax.fori_loop(0, size // GROUP, some, 0)

    def do_l(i):
        raw_center(flows_l[i])
        for flow in on_l[i]:
            start(*flow)
        start_center(flows_x[i])
        if i == NC - 1:
            for later in flows_x:
                start_edges(later)
        raw_edges(flows_l[i])
        for flow in on_l[i]:
            arrive(*flow)

    def do_a(i):
        def body(l):
            a_buf[l] = ad_model(ring_l, l)
        for_levels(i, body)
        start(*down_a[i])

    def do_e(i):
        raw_center(flows_x[i])
        for flow in on_x[i]:
            start(*flow)

        def body(l):
            e_buf[l] = dl[l] + ring_x[l, 0:rows, :]
        for_levels(i, body)
        start(*down_e[i])

    def do_p(i):
        arrive(*down_a[i])

        def body(l):
            ring_p[l, 0:rows, :] = ring_l[l, 0:rows, :] - a_in[l] + ht[l]
        for_levels(i, body)
        for flow in halo_p[i]:
            start(*flow)

    def do_m(i):
        raw_edges(flows_x[i])
        for flow in on_x[i]:
            arrive(*flow)

        def body(l):
            m_buf[l] = jnp.where(not_last_k, tl_model(ring_x, l), 0.0)
        for_levels(i, body)

    def do_q(i):
        arrive(*down_e[i])

        def body(l):
            ring_q[l, 0:rows, :] = e_in[l] - m_buf[l]
        for_levels(i, body)
        for flow in halo_q[i]:
            start(*flow)

    def do_n(i):
        for flow in halo_p[i]:
            arrive(*flow)

        def body(l):
            n_buf[l] = jnp.where(not_first_k, tl_model(ring_p, l), 0.0)
        for_levels(i, body)

    def do_b(i):
        for flow in halo_q[i]:
            arrive(*flow)

        def body(l):
            b_buf[l] = ad_model(ring_q, l)
        for_levels(i, body)
        start(*down_b[i])

    def do_ol(i):
        arrive(*down_p[i])

        def body(l):
            ol_buf[l] = dl[l] + (d2_in[l] - n_buf[l])
        for_levels(i, body)
        start(*out_l[i])
        home(*out_l[i][1:], "start")

    def do_ox(i):
        arrive(*down_b[i])

        def body(l):
            ox_buf[l] = ring_q[l, 0:rows, :] - b_in[l] + ht[l]
        for_levels(i, body)
        start(*out_x[i])
        home(*out_x[i][1:], "start")

    for i in range(NC):
        do_l(i)
        if i < NC - 1:
            do_a(i)
    vertical(ring_l, store_dl)
    for i in range(NC):
        do_e(i)
    do_a(NC - 1)
    for i in range(NC):
        if i > 0:
            do_m(i - 1)
        do_p(i)
    do_m(NC - 1)
    for i in range(NC):
        start(*down_p[i])
    arrive(*fresh_0)
    arrive(*fresh_1)

    @pl.when(fresh_own)
    def _():
        pltpu.make_async_copy(fresh.at[0], e_in, rsem.at[SLOT["F0"]]).wait()
        pltpu.make_async_copy(fresh.at[1], d2_in, rsem.at[SLOT["F1"]]).wait()
    for i in range(NC):
        do_q(i)
    mu_buf[...] = jnp.broadcast_to(var * mu + sampled(ring_x[:, 0:rows, :]), mu_buf.shape)
    start(*down_mu)

    @pl.when(jnp.logical_not(not_last_k))
    def _():
        mu_in[...] = jnp.broadcast_to(aux_in[1:2, :], mu_in.shape)

    for i in range(NC):
        do_n(i)
        if i == NC - 1:
            arrive(*down_mu)
            mu_two = mu_in[0:1, :]
            spread(mu_two)
        do_b(i)
    do_ox(0)
    vertical(ring_q, store_dl)
    for i in range(NC):
        do_ol(i)
    oo_buf[...] = var * mu_two + sampled(d2_in[...])
    start(*out_o)

    @pl.when(jnp.logical_not(swapped))
    def _():
        out_obs[...] = oo_buf[...]

    for i in range(1, NC):
        do_ox(i)

    everything = [flow_aux, fresh_0, fresh_1, down_mu, out_o, *flows_c]
    for group in (*flows_l, *flows_x, *on_l, *on_x, *halo_p, *halo_q):
        everything += list(group)
    everything += down_a + down_e + down_p + down_b + out_l + out_x
    for flow in everything:
        sent(*flow)
    for flow in (*out_l, *out_x):
        arrive(*flow)
        home(*flow[1:], "wait")
    arrive(*out_o)


def hand_over(*refs):
    sources, targets, stops, sems = refs[:3], refs[3:6], refs[6:9], refs[9]
    inward, outward = [], []
    for source, target, stop in zip(sources, targets, stops):
        pieces = 3 if len(source.shape) == 3 else 1
        step = source.shape[0] // pieces
        for i in range(pieces):
            span, n = pl.ds(i * step, step), len(inward)
            inward.append(pltpu.make_async_copy(source.at[span], stop.at[span], sems.at[0, n]))
            outward.append(pltpu.make_async_copy(stop.at[span], target.at[span], sems.at[1, n]))
    for copy in inward:
        copy.start()
    for first, second in zip(inward, outward):
        first.wait()
        second.start()
    for copy in outward:
        copy.wait()


def local(
    lam,
    obs_mult,
    dx,
    fresh_state,
    fresh_obs,
    sigma,
    obs_var,
    obs_idx,
    stencil_coef,
    vert_cov,
    block_pattern,
):
    field = dx.shape[1:]
    levels, rows, cols = field
    nobs = obs_mult.shape[1]
    ring = (levels, 2 * rows, cols)
    deep = -(-levels // 16) * 16
    anywhere, vmem = pl.BlockSpec(memory_space=pl.ANY), pl.BlockSpec(memory_space=pltpu.VMEM)
    out_lam, out_obs, out_dx = pl.pallas_call(
        kernel,
        name="saddle_slide",
        out_shape=(
            jax.ShapeDtypeStruct(field, F32),
            jax.ShapeDtypeStruct((1, nobs), F32),
            jax.ShapeDtypeStruct(field, F32),
        ),
        in_specs=[anywhere] * 11,
        out_specs=(anywhere, vmem, anywhere),
        scratch_shapes=[
            *[pltpu.VMEM(ring, F32)] * 4,
            pltpu.VMEM((3, 2 * rows, cols), F32),
            pltpu.VMEM((2 * rows, cols), F32),
            *[pltpu.VMEM(field, F32)] * 13,
            pltpu.VMEM((8, nobs), F32),
            pltpu.VMEM((8, nobs), F32),
            pltpu.VMEM((8, nobs), F32),
            pltpu.VMEM((8, nobs), F32),
            pltpu.VMEM((1, nobs), F32),
            pltpu.VMEM((levels, 3 * deep), BF16),
            pltpu.VMEM((levels * rows, nobs), BF16),
            pltpu.VMEM((1, nobs), F32),
            pltpu.VMEM((1, nobs), F32),
            pltpu.VMEM((1, levels), F32),
            pltpu.VMEM((1, nobs), F32),
            pltpu.VMEM((1, nobs), jnp.int32),
            pltpu.VMEM(vert_cov.shape, F32),
            pltpu.VMEM(block_pattern.shape, jnp.int32),
            pltpu.SemaphoreType.DMA((NSEM,)),
            pltpu.SemaphoreType.DMA((NSEM,)),
            pltpu.SemaphoreType.DMA((7,)),
        ],
        compiler_params=pltpu.CompilerParams(
            collective_id=0, has_side_effects=True, vmem_limit_bytes=63 * 2**20
        ),
        cost_estimate=pl.CostEstimate(flops=10**9, bytes_accessed=5 * 10**6, transcendentals=0),
    )(
        lam[0],
        obs_mult,
        dx[0],
        fresh_state,
        fresh_obs[None],
        sigma,
        obs_var[None],
        obs_idx[None],
        stencil_coef,
        vert_cov,
        block_pattern,
    )
    results = (out_lam, out_obs, out_dx)
    out_lam, out_obs, out_dx = pl.pallas_call(
        hand_over,
        name="hand_over",
        out_shape=tuple(jax.ShapeDtypeStruct(r.shape, r.dtype) for r in results),
        in_specs=[anywhere] * 3,
        out_specs=(anywhere,) * 3,
        scratch_shapes=[
            *[pltpu.VMEM(r.shape, r.dtype) for r in results],
            pltpu.SemaphoreType.DMA((2, 7)),
        ],
        compiler_params=pltpu.CompilerParams(vmem_limit_bytes=63 * 2**20),
    )(*results)
    return out_lam[None], out_obs, out_dx[None]


def solution(mesh):
    in_specs = (
        P("tm", None, "space", None),
        P("tm", "space"),
        P("tm", None, "space", None),
        P(None, None, "space", None),
        P("space"),
        P("tm", None),
        P("space"),
        P("space"),
        P(None, "space", None),
        P(),
        P(),
    )
    out_specs = (P("tm", None, "space", None), P("tm", "space"), P("tm", None, "space", None))
    return jax.shard_map(local, mesh=mesh, in_specs=in_specs, out_specs=out_specs, check_vma=False)
```
